32 devices in a mesh: segment: 2 (over y), lon: 4 (over x, core), lat: 4 (over z).
Axes of the slice: x: 2, y: 2, z: 4, core: 2. Of those that a mesh axis runs over, the one named last changes fastest.
Arguments:
- latents: bfloat16 [2, 24, 48, 1024], P(None, 'lat', 'lon'), may hold values from -48 to 48
- land_mask: int32 [24, 48], P('lat', 'lon'), may hold values 0 or 1
- land_embed: bfloat16 [1024], replicated, may hold values from -6 to 6
- qkv_weight: bfloat16 [2, 1024, 3072], P('segment'), may hold values from -0.25625 to 0.25625
- out_weight: bfloat16 [2, 1024, 1024], P('segment'), may hold values from -0.5625 to 0.5625
- norm_gain: float32 [2, 1024], replicated, may hold values from 0.5 to 1.5
- offsets: int32 [2, 2], replicated, may hold values from 0 to 11, as said below
Outputs:
- sections: bfloat16 [2, 2, 24, 48, 1024], P('segment', None, 'lat', 'lon')
The draws below stay inside these ranges and needn't reach their ends.
Inputs may be any that keep to these rules, and one draw needn't show every extreme that they name: offsets[s, 0] lies in 0 to 5 and offsets[s, 1] in 0 to 11; one of the two sections has offsets[s, 0] = 5 and offsets[s, 1] = 11.
All inputs are finite; a program needn't handle non-finite values. No bound on the sum of `land_mask` on one device may be relied on, other than what follows from the above.
Results may differ from the reference program's by a relative error of at most 0.015.
Values may be sent and summed in bfloat16 or wider, within the bound.
A program may use at most 64 MiB of HBM per device.

```python
import math
import jax
import jax.numpy as jnp
from jax import lax

D = 1024
HEADS = 16
HEAD = 64
WLAT = 6
WLON = 12
LB = 2
NLAT = 24
NLON = 48


def draw_latents(key, part):
    base_key = jax.random.fold_in(jax.random.fold_in(key, 11), 0)
    values = jnp.clip(jax.random.normal(base_key, (LB, NLAT, NLON, D), jnp.float32), -6.0, 6.0)
    return values.astype(jnp.bfloat16)


def draw_qkv_weight(key, part):
    first_key, second_key, third_key = jax.random.split(jax.random.fold_in(key, 23), 3)
    scale = D ** (-0.5)
    shared = jnp.clip(jax.random.normal(first_key, (2, D, D), jnp.float32), -6.0, 6.0)
    apart = jnp.clip(jax.random.normal(second_key, (2, D, D), jnp.float32), -6.0, 6.0)
    valued = jnp.clip(jax.random.normal(third_key, (2, D, D), jnp.float32), -6.0, 6.0)
    query_part = shared * scale
    key_part = (0.5 * shared + 0.866 * apart) * scale
    value_part = valued * scale
    return jnp.concatenate([query_part, key_part, value_part], axis=2).astype(jnp.bfloat16)


def draw_out_weight(key, part):
    base_key, column_key = jax.random.split(jax.random.fold_in(key, 37))
    values = jnp.clip(jax.random.normal(base_key, (2, D, D), jnp.float32), -6.0, 6.0)
    column_scale = jnp.exp(jax.random.uniform(column_key, (2, 1, D), minval=math.log(0.3), maxval=math.log(3.0)))
    return (values * D ** (-0.5) * column_scale).astype(jnp.bfloat16)


def draw_offsets(key, part):
    lat_key, lon_key, pick_key = jax.random.split(jax.random.fold_in(key, 41), 3)
    lat_shift = jax.random.randint(lat_key, (2,), 0, WLAT)
    lon_shift = jax.random.randint(lon_key, (2,), 0, WLON)
    chosen = jax.random.randint(pick_key, (), 0, 2)
    segment_ids = jnp.arange(2, dtype=jnp.int32)
    lat_shift = jnp.where(segment_ids == chosen, WLAT - 1, lat_shift)
    lon_shift = jnp.where(segment_ids == chosen, WLON - 1, lon_shift)
    return jnp.stack([lat_shift, lon_shift], axis=1).astype(jnp.int32)


def with_ends(entries, key, low, largest):
    index_at = [jax.random.randint(jax.random.fold_in(key, axis), (), 0, length) for axis, length in enumerate(entries.shape)]
    longest = entries.shape.index(max(entries.shape))
    next_to = index_at[:longest] + [(index_at[longest] + 1) % entries.shape[longest]] + index_at[longest + 1:]
    return entries.at[tuple(index_at)].set(low).at[tuple(next_to)].set(largest)


def normal_values(stream_key, extent, deviation, reach, held_as=jnp.bfloat16):
    entries = deviation * jax.random.normal(stream_key, extent, jnp.float32)
    return jnp.clip(entries, min=-reach, max=reach).astype(held_as)


def setup_inputs(seed: int = 0) -> dict:
    key_list = jax.random.split(jax.random.key(seed), 8)
    return {
        "latents": draw_latents(jax.random.fold_in(key_list[7], 71), 0),
        "land_mask": with_ends((jax.random.randint(key_list[1], (NLAT, NLON), 0, 10) < 3).astype(jnp.int32), jax.random.fold_in(key_list[1], 1), 0, 1),
        "land_embed": normal_values(key_list[2], (D,), 1.0, 6.0),
        "qkv_weight": draw_qkv_weight(jax.random.fold_in(key_list[7], 71), 0),
        "out_weight": draw_out_weight(jax.random.fold_in(key_list[7], 71), 0),
        "norm_gain": jnp.clip(1.0 + 0.1 * jax.random.normal(key_list[5], (2, D), jnp.float32), 0.5, 1.5),
        "offsets": draw_offsets(jax.random.fold_in(key_list[7], 71), 0),
    }


def run_section(field, wqkv, wout, gain, lat_offset, lon_offset):
    total_rows, total_cols, width = field.shape
    cell_count = WLAT * WLON
    rolled = jnp.roll(field, (-lat_offset, -lon_offset), (0, 1))
    row_windows = total_rows // WLAT
    col_windows = total_cols // WLON
    cells = rolled.reshape(row_windows, WLAT, col_windows, WLON, width).transpose(0, 2, 1, 3, 4)
    cells = cells.reshape(row_windows, col_windows, cell_count, width)
    wrapped = jnp.arange(total_rows, dtype=jnp.int32) + lat_offset >= total_rows
    flags = jnp.broadcast_to(wrapped.reshape(row_windows, 1, WLAT, 1), (row_windows, col_windows, WLAT, WLON))
    flags = flags.reshape(row_windows, col_windows, cell_count)

    def one_row(pair):
        row_cells, row_flags = pair
        flat = row_cells.reshape(-1, width)
        packed = jnp.dot(flat, wqkv, preferred_element_type=jnp.float32).astype(jnp.bfloat16)
        packed = packed.reshape(col_windows, cell_count, 3, HEADS, HEAD)
        queries = packed[:, :, 0].astype(jnp.float32)
        keys = packed[:, :, 1].astype(jnp.float32)
        values = packed[:, :, 2].astype(jnp.float32)
        scores = jnp.einsum('nqhd,nkhd->nhqk', queries, keys) / math.sqrt(HEAD)
        allowed = row_flags[:, :, None] == row_flags[:, None, :]
        scores = jnp.where(allowed[:, None], scores, -1e+30)
        probs = jax.nn.softmax(scores, axis=-1).astype(jnp.bfloat16)
        attended = jnp.einsum('nhqk,nkhd->nqhd', probs.astype(jnp.float32), values)
        attended = attended.astype(jnp.bfloat16).reshape(-1, width)
        projected = jnp.dot(attended, wout, preferred_element_type=jnp.float32)
        centered = projected - lax.optimization_barrier(jnp.mean(projected, axis=-1, keepdims=True))
        variance = lax.optimization_barrier(jnp.mean(centered * centered, axis=-1, keepdims=True))
        branch = centered * lax.rsqrt(variance + 1e-05) * gain
        summed = (flat.astype(jnp.float32) + branch).astype(jnp.bfloat16)
        return summed.reshape(col_windows, cell_count, width)
    result = lax.map(one_row, (cells, flags))
    grid = result.reshape(row_windows, col_windows, WLAT, WLON, width).transpose(0, 2, 1, 3, 4)
    grid = grid.reshape(total_rows, total_cols, width)
    return jnp.roll(grid, (lat_offset, lon_offset), (0, 1))

def reference(latents, land_mask, land_embed, qkv_weight, out_weight, norm_gain, offsets):
    land_term = land_mask.astype(jnp.float32)[:, :, None] * land_embed.astype(jnp.float32)
    first_list = []
    second_list = []
    for block_index in range(LB):
        seeded = (latents[block_index].astype(jnp.float32) + land_term).astype(jnp.bfloat16)
        first_out = run_section(seeded, qkv_weight[0], out_weight[0], norm_gain[0], offsets[0, 0], offsets[0, 1])
        second_out = run_section(first_out, qkv_weight[1], out_weight[1], norm_gain[1], offsets[1, 0], offsets[1, 1])
        first_list.append(first_out)
        second_list.append(second_out)
    return jnp.stack([jnp.stack(first_list), jnp.stack(second_list)])
```

```python
import functools
import math

import jax
import jax.numpy as jnp
from jax import lax
from jax.experimental import pallas as pl
from jax.experimental.pallas import tpu as pltpu
from jax.sharding import PartitionSpec as P

HEADS = 16
WLAT = 6
WLON = 12
HALF_LAT = WLAT // 2
HALF_LON = WLON // 2
STEPS = 4
PAIR = 128
NT = (((1,), (1,)), ((), ()))


def attend_kernel(col_code, row_code, x_ref, wq_ref, wk_ref, wv_ref, wo_ref, gain_ref, out_ref, total, *, head_size):
    step = pl.program_id(0)
    x = x_ref[...]
    q = jnp.dot(x, wq_ref[...], preferred_element_type=jnp.float32).astype(jnp.bfloat16)
    k = jnp.dot(x, wk_ref[...], preferred_element_type=jnp.float32).astype(jnp.bfloat16)
    v = jnp.dot(x, wv_ref[...], preferred_element_type=jnp.float32).astype(jnp.bfloat16)
    allowed = col_code[...] == row_code[...]
    scale = 1.0 / math.sqrt(head_size)
    first_half = lax.broadcasted_iota(jnp.int32, (x.shape[0], PAIR), 1) < head_size
    parts = []
    for pair in range(q.shape[1] // PAIR):
        columns = slice(pair * PAIR, (pair + 1) * PAIR)
        q2, k2, v2 = q[:, columns], k[:, columns], v[:, columns]
        weighted = []
        for keep in (first_half, ~first_half):
            qh = jnp.where(keep, q2, jnp.zeros_like(q2))
            scores = lax.dot_general(qh, k2, NT, preferred_element_type=jnp.float32) * scale
            scores = jnp.where(allowed, scores, -1e30)
            weights = jnp.exp(scores - jnp.max(scores, axis=-1, keepdims=True))
            inverse = 1.0 / jnp.sum(weights, axis=-1, keepdims=True)
            probs = (weights * inverse).astype(jnp.bfloat16)
            weighted.append(jnp.dot(probs, v2, preferred_element_type=jnp.float32))
        parts.append(jnp.where(first_half, weighted[0], weighted[1]).astype(jnp.bfloat16))
    attended = jnp.concatenate(parts, axis=1)
    projected = jnp.dot(attended, wo_ref[...], preferred_element_type=jnp.float32)

    @pl.when(step == 0)
    def _():
        total[...] = projected

    @pl.when(step > 0)
    def _():
        total[...] += projected

    @pl.when(step == STEPS - 1)
    def _():
        whole = total[...]
        centered = whole - jnp.mean(whole, axis=-1, keepdims=True)
        variance = jnp.mean(centered * centered, axis=-1, keepdims=True)
        branch = centered * lax.rsqrt(variance + 1e-05) * gain_ref[...]
        out_ref[...] = (x.astype(jnp.float32) + branch).astype(jnp.bfloat16)


def attend(field, codes, wqkv, wout, gain):
    width = field.shape[-1]
    flat = field.reshape(-1, width)
    cells = flat.shape[0]
    slab = width // STEPS
    head_size = width // HEADS
    full = lambda shape: pl.BlockSpec(shape, lambda p: (0, 0))
    out = pl.pallas_call(
        functools.partial(attend_kernel, head_size=head_size),
        grid=(STEPS,),
        out_shape=jax.ShapeDtypeStruct((cells, width), jnp.bfloat16),
        in_specs=[
            full((cells, 1)),
            full((1, cells)),
            full((cells, width)),
            pl.BlockSpec((width, slab), lambda p: (0, p)),
            pl.BlockSpec((width, slab), lambda p: (0, p + STEPS)),
            pl.BlockSpec((width, slab), lambda p: (0, p + 2 * STEPS)),
            pl.BlockSpec((slab, width), lambda p: (p, 0)),
            full((1, width)),
        ],
        out_specs=full((cells, width)),
        scratch_shapes=[pltpu.VMEM((cells, width), jnp.float32)],
        compiler_params=pltpu.CompilerParams(vmem_limit_bytes=24 * 1024 * 1024),
        cost_estimate=pl.CostEstimate(
            flops=8 * cells * width * width, bytes_accessed=8 * width * width, transcendentals=HEADS * cells * cells
        ),
    )(codes[:, None], codes[None, :], flat, wqkv, wqkv, wqkv, wout, gain[None, :])
    return out.reshape(field.shape)


def moved(piece, lat_steps, lon_steps):
    segments, lons, lats = (lax.axis_size(axis) for axis in ("segment", "lon", "lat"))
    place = lambda s, j, i: (s * lons + j % lons) * lats + i % lats
    route = [
        (place(s, j + lon_steps[s], i + lat_steps[s]), place(s, j, i))
        for s in range(segments)
        for j in range(lons)
        for i in range(lats)
    ]
    return lax.ppermute(piece, ("segment", "lon", "lat"), route)


def by_segment(make, steps):
    if steps[0] == steps[1]:
        return make(steps[0])
    return jnp.where(lax.axis_index("segment") == 0, make(steps[0]), make(steps[1]))


def shift_one_way(lat_steps, lon_steps, field, lat_shift, lon_shift):
    rows = lambda step: field[:, :HALF_LAT] if step > 0 else field[:, WLAT - HALF_LAT:]
    columns = lambda part: lambda step: part[:, :, :HALF_LON] if step > 0 else part[:, :, WLON - HALF_LON:]
    still = (0, 0)
    row_piece = by_segment(rows, lat_steps)
    below = moved(row_piece, lat_steps, still)
    corner = moved(by_segment(columns(row_piece), lon_steps), lat_steps, lon_steps)
    beside = moved(by_segment(columns(field), lon_steps), still, lon_steps)
    block_count, row_count, column_count, width = field.shape

    def joined(own, other, axis, start, half, size):
        def make(step):
            pair = [own, other] if step > 0 else [other, own]
            return lax.dynamic_slice_in_dim(
                jnp.concatenate(pair, axis=axis), start if step > 0 else half + start, size, axis
            )

        return make

    near = by_segment(joined(field, beside, 2, lon_shift, HALF_LON, column_count), lon_steps)
    far = by_segment(joined(below, corner, 2, lon_shift, HALF_LON, column_count), lon_steps)
    return by_segment(joined(near, far, 1, lat_shift, HALF_LAT, row_count), lat_steps)


def shift(field, lat_shift, lon_shift):
    choice = 2 * (lat_shift < 0).astype(jnp.int32) + (lon_shift < 0).astype(jnp.int32)
    ways = [functools.partial(shift_one_way, (a, a), (b, b)) for a in (1, -1) for b in (1, -1)]
    return lax.switch(choice, ways, field, lat_shift, lon_shift)


def shift_each(field, lat_shifts, lon_shifts):
    other = jnp.where((lat_shifts[1] < 0) | (lon_shifts[1] < 0), 1, 0)
    lat_other, lon_other = lat_shifts[other], lon_shifts[other]
    choice = 4 * other + 2 * (lat_other < 0).astype(jnp.int32) + (lon_other < 0).astype(jnp.int32)
    ways = []
    for segment in (0, 1):
        for a in (1, -1):
            for b in (1, -1):
                lat_steps = (a, 1) if segment == 0 else (1, a)
                lon_steps = (b, 1) if segment == 0 else (1, b)
                ways.append(functools.partial(shift_one_way, lat_steps, lon_steps))
    own = lax.axis_index("segment")
    return lax.switch(choice, ways, field, lat_shifts[own], lon_shifts[own])


def body(latents, land_mask, land_embed, qkv_weight, out_weight, norm_gain, offsets):
    segment_index = lax.axis_index("segment")
    block_count, row_count, column_count, width = latents.shape
    assert (row_count, column_count) == (WLAT, WLON)
    total_rows = row_count * lax.axis_size("lat")
    land_term = land_mask.astype(jnp.float32)[None, :, :, None] * land_embed.astype(jnp.float32)
    seeded = (latents.astype(jnp.float32) + land_term).astype(jnp.bfloat16)
    wqkv = qkv_weight[0]
    wout = out_weight[0]
    gain = lax.dynamic_index_in_dim(norm_gain, segment_index, 0, False)
    lat_offset, lon_offset = offsets[:, 0], offsets[:, 1]
    lat_base = jnp.where(lat_offset >= HALF_LAT, lat_offset - WLAT, lat_offset)
    lon_base = jnp.where(lon_offset >= HALF_LON, lon_offset - WLON, lon_offset)

    def codes_of(s):
        held = lax.axis_index("lat") * row_count + jnp.arange(row_count, dtype=jnp.int32) + lat_base[s]
        wrapped = (held % total_rows < lat_offset[s]).astype(jnp.int32)
        blocks = 2 * jnp.arange(block_count, dtype=jnp.int32)
        codes = jnp.broadcast_to(
            blocks[:, None, None] + wrapped[None, :, None], (block_count, row_count, column_count)
        )
        return codes.reshape(-1)

    first_in = shift(seeded, lat_base[0], lon_base[0])
    first = attend(first_in, codes_of(0), wqkv, wout, gain)
    passed = lax.ppermute(first, "segment", [(0, 1)])
    second_in = shift(passed, lat_base[1] - lat_base[0], lon_base[1] - lon_base[0])
    second = attend(second_in, codes_of(1), wqkv, wout, gain)
    merged = jnp.where(segment_index == 0, first, second)
    return shift_each(merged, -lat_base, -lon_base)[None]


def solution(mesh):
    return jax.shard_map(
        body,
        mesh=mesh,
        in_specs=(
            P(None, "lat", "lon", None),
            P("lat", "lon"),
            P(),
            P("segment", None, None),
            P("segment", None, None),
            P(),
            P(),
        ),
        out_specs=P("segment", None, "lat", "lon", None),
        check_vma=False,
    )
```

```python
import functools
import math

import jax
import jax.numpy as jnp
from jax import lax
from jax.experimental import pallas as pl
from jax.experimental.pallas import tpu as pltpu
from jax.sharding import PartitionSpec as P

HEADS = 16
WLAT = 6
WLON = 12
HALF_LAT = WLAT // 2
HALF_LON = WLON // 2
STEPS = 4
PAIR = 128
NT = (((1,), (1,)), ((), ()))


def cell_codes(place_ref, shape, axis, total_rows):
    cell = lax.broadcasted_iota(jnp.int32, shape, axis)
    line = jnp.zeros(shape, jnp.int32)
    for start in range(WLON, shape[axis], WLON):
        line += (cell >= start).astype(jnp.int32)
    block = jnp.zeros(shape, jnp.int32)
    for start in range(WLAT, shape[axis] // WLON, WLAT):
        block += (line >= start).astype(jnp.int32)
    held = place_ref[0] + line - WLAT * block
    held = jnp.where(held < 0, held + total_rows, held)
    held = jnp.where(held >= total_rows, held - total_rows, held)
    return 2 * block + (held < place_ref[1]).astype(jnp.int32)


def attend_kernel(place_ref, x_ref, wq_ref, wk_ref, wv_ref, wo_ref, gain_ref, out_ref, total, *, head_size, total_rows):
    step = pl.program_id(0)
    x = x_ref[...]
    q = jnp.dot(x, wq_ref[...], preferred_element_type=jnp.float32).astype(jnp.bfloat16)
    k = jnp.dot(x, wk_ref[...], preferred_element_type=jnp.float32).astype(jnp.bfloat16)
    v = jnp.dot(x, wv_ref[...], preferred_element_type=jnp.float32).astype(jnp.bfloat16)
    cells = x.shape[0]
    allowed = (
        cell_codes(place_ref, (cells, 1), 0, total_rows) == cell_codes(place_ref, (1, cells), 1, total_rows)
    )
    scale = 1.0 / math.sqrt(head_size)
    first_half = lax.broadcasted_iota(jnp.int32, (x.shape[0], PAIR), 1) < head_size
    parts = []
    for pair in range(q.shape[1] // PAIR):
        columns = slice(pair * PAIR, (pair + 1) * PAIR)
        q2, k2, v2 = q[:, columns], k[:, columns], v[:, columns]
        weighted = []
        for keep in (first_half, ~first_half):
            qh = jnp.where(keep, q2, jnp.zeros_like(q2))
            scores = lax.dot_general(qh, k2, NT, preferred_element_type=jnp.float32) * scale
            scores = jnp.where(allowed, scores, -1e30)
            weights = jnp.exp(scores - jnp.max(scores, axis=-1, keepdims=True))
            inverse = 1.0 / jnp.sum(weights, axis=-1, keepdims=True)
            probs = (weights * inverse).astype(jnp.bfloat16)
            weighted.append(jnp.dot(probs, v2, preferred_element_type=jnp.float32))
        parts.append(jnp.where(first_half, weighted[0], weighted[1]).astype(jnp.bfloat16))
    attended = jnp.concatenate(parts, axis=1)
    projected = jnp.dot(attended, wo_ref[...], preferred_element_type=jnp.float32)

    @pl.when(step == 0)
    def _():
        total[...] = projected

    @pl.when(step > 0)
    def _():
        total[...] += projected

    @pl.when(step == STEPS - 1)
    def _():
        whole = total[...]
        centered = whole - jnp.mean(whole, axis=-1, keepdims=True)
        variance = jnp.mean(centered * centered, axis=-1, keepdims=True)
        branch = centered * lax.rsqrt(variance + 1e-05) * gain_ref[...]
        out_ref[...] = (x.astype(jnp.float32) + branch).astype(jnp.bfloat16)


def attend(field, place, wqkv, wout, gain):
    width = field.shape[-1]
    flat = field.reshape(-1, width)
    cells = flat.shape[0]
    slab = width // STEPS
    head_size = width // HEADS
    full = lambda shape: pl.BlockSpec(shape, lambda p: (0, 0))
    out = pl.pallas_call(
        functools.partial(
            attend_kernel, head_size=head_size, total_rows=WLAT * lax.axis_size("lat")
        ),
        grid=(STEPS,),
        out_shape=jax.ShapeDtypeStruct((cells, width), jnp.bfloat16),
        in_specs=[
            pl.BlockSpec(memory_space=pltpu.SMEM),
            full((cells, width)),
            pl.BlockSpec((width, slab), lambda p: (0, p)),
            pl.BlockSpec((width, slab), lambda p: (0, p + STEPS)),
            pl.BlockSpec((width, slab), lambda p: (0, p + 2 * STEPS)),
            pl.BlockSpec((slab, width), lambda p: (p, 0)),
            full((1, width)),
        ],
        out_specs=full((cells, width)),
        scratch_shapes=[pltpu.VMEM((cells, width), jnp.float32)],
        compiler_params=pltpu.CompilerParams(vmem_limit_bytes=56 * 1024 * 1024),
        cost_estimate=pl.CostEstimate(
            flops=8 * cells * width * width, bytes_accessed=8 * width * width, transcendentals=HEADS * cells * cells
        ),
    )(place, flat, wqkv, wqkv, wqkv, wout, gain[None, :])
    return out.reshape(field.shape)


def exchange_kernel(lat_steps, lon_steps, below_in, corner_in, beside_in, below, corner, beside, send_sem, recv_sem):
    segment, lon, lat = (lax.axis_index(axis) for axis in ("segment", "lon", "lat"))
    lons, lats = lax.axis_size("lon"), lax.axis_size("lat")
    pick = lambda steps: steps[0] + segment * (steps[1] - steps[0])
    lat_step, lon_step = pick(lat_steps), pick(lon_steps)
    place = lambda a, b: (segment, lax.rem(lon + b + lons, lons), lax.rem(lat + a + lats, lats))
    ways = ((lat_step, lon_step), (lat_step, 0), (0, lon_step))
    barrier = pltpu.get_barrier_semaphore()
    for a, b in ways:
        pl.semaphore_signal(barrier, inc=1, device_id=place(a, b), device_id_type=pl.DeviceIdType.MESH)
    pl.semaphore_wait(barrier, 3)
    copies = []
    for index, ((a, b), source, target) in enumerate(
        zip(ways, (corner_in, below_in, beside_in), (corner, below, beside))
    ):
        copy = pltpu.make_async_remote_copy(
            src_ref=source,
            dst_ref=target,
            send_sem=send_sem.at[index],
            recv_sem=recv_sem.at[index],
            device_id=place(-a, -b),
            device_id_type=pl.DeviceIdType.MESH,
        )
        copy.start()
        copies.append(copy)
    for copy in copies:
        copy.wait()


def exchanged(lat_steps, lon_steps, pieces):
    width = pieces[0].shape[-1]
    flats = []
    for piece in pieces:
        flat = piece.reshape(-1, width)
        flats.append(jnp.pad(flat, ((0, -flat.shape[0] % 16), (0, 0))))
    signs = [(1, 1), (1, -1), (-1, 1), (-1, -1)]
    in_vmem = pl.BlockSpec(memory_space=pltpu.VMEM)
    results = pl.pallas_call(
        functools.partial(exchange_kernel, lat_steps, lon_steps),
        out_shape=[jax.ShapeDtypeStruct(flat.shape, flat.dtype) for flat in flats],
        in_specs=[in_vmem] * 3,
        out_specs=[in_vmem] * 3,
        scratch_shapes=[pltpu.SemaphoreType.DMA((3,)), pltpu.SemaphoreType.DMA((3,))],
        compiler_params=pltpu.CompilerParams(
            collective_id=4 * signs.index(lat_steps) + signs.index(lon_steps),
            has_side_effects=True,
            vmem_limit_bytes=8 * 1024 * 1024,
        ),
    )(*flats)
    return [out[: math.prod(piece.shape[:-1])].reshape(piece.shape) for out, piece in zip(results, pieces)]


def by_segment(make, steps):
    if steps[0] == steps[1]:
        return make(steps[0])
    return jnp.where(lax.axis_index("segment") == 0, make(steps[0]), make(steps[1]))


def shift_one_way(lat_steps, lon_steps, field, lat_shift, lon_shift):
    rows = lambda step: field[:, :HALF_LAT] if step > 0 else field[:, WLAT - HALF_LAT:]
    columns = lambda part: lambda step: part[:, :, :HALF_LON] if step > 0 else part[:, :, WLON - HALF_LON:]
    row_piece = by_segment(rows, lat_steps)
    corner_piece = by_segment(columns(row_piece), lon_steps)
    column_piece = by_segment(columns(field), lon_steps)
    below, corner, beside = exchanged(lat_steps, lon_steps, (row_piece, corner_piece, column_piece))
    block_count, row_count, column_count, width = field.shape

    def joined(own, other, axis, start, half, size):
        def make(step):
            pair = [own, other] if step > 0 else [other, own]
            return lax.dynamic_slice_in_dim(
                jnp.concatenate(pair, axis=axis), start if step > 0 else half + start, size, axis
            )

        return make

    near = by_segment(joined(field, beside, 2, lon_shift, HALF_LON, column_count), lon_steps)
    far = by_segment(joined(below, corner, 2, lon_shift, HALF_LON, column_count), lon_steps)
    return by_segment(joined(near, far, 1, lat_shift, HALF_LAT, row_count), lat_steps)


def shift(field, lat_shift, lon_shift):
    choice = 2 * (lat_shift < 0).astype(jnp.int32) + (lon_shift < 0).astype(jnp.int32)
    ways = [functools.partial(shift_one_way, (a, a), (b, b)) for a in (1, -1) for b in (1, -1)]
    return lax.switch(choice, ways, field, lat_shift, lon_shift)


def shift_each(field, lat_shifts, lon_shifts):
    other = jnp.where((lat_shifts[1] < 0) | (lon_shifts[1] < 0), 1, 0)
    lat_other, lon_other = lat_shifts[other], lon_shifts[other]
    choice = 4 * other + 2 * (lat_other < 0).astype(jnp.int32) + (lon_other < 0).astype(jnp.int32)
    ways = []
    for segment in (0, 1):
        for a in (1, -1):
            for b in (1, -1):
                lat_steps = (a, 1) if segment == 0 else (1, a)
                lon_steps = (b, 1) if segment == 0 else (1, b)
                ways.append(functools.partial(shift_one_way, lat_steps, lon_steps))
    own = lax.axis_index("segment")
    return lax.switch(choice, ways, field, lat_shifts[own], lon_shifts[own])


def body(latents, land_mask, land_embed, qkv_weight, out_weight, norm_gain, offsets):
    segment_index = lax.axis_index("segment")
    row_count, column_count = latents.shape[1:3]
    assert (row_count, column_count) == (WLAT, WLON)
    land_term = land_mask.astype(jnp.float32)[None, :, :, None] * land_embed.astype(jnp.float32)
    seeded = (latents.astype(jnp.float32) + land_term).astype(jnp.bfloat16)
    wqkv = qkv_weight[0]
    wout = out_weight[0]
    gain = lax.dynamic_index_in_dim(norm_gain, segment_index, 0, False)
    lat_offset, lon_offset = offsets[:, 0], offsets[:, 1]
    lat_base = jnp.where(lat_offset >= HALF_LAT, lat_offset - WLAT, lat_offset)
    lon_base = jnp.where(lon_offset >= HALF_LON, lon_offset - WLON, lon_offset)

    def place_of(s):
        return jnp.stack([lax.axis_index("lat") * row_count + lat_base[s], lat_offset[s]])

    first_in = shift(seeded, lat_base[0], lon_base[0])
    first = attend(first_in, place_of(0), wqkv, wout, gain)
    passed = lax.ppermute(first, "segment", [(0, 1)])
    second_in = shift(passed, lat_base[1] - lat_base[0], lon_base[1] - lon_base[0])
    second = attend(second_in, place_of(1), wqkv, wout, gain)
    merged = jnp.where(segment_index == 0, first, second)
    return shift_each(merged, -lat_base, -lon_base)[None]


def solution(mesh):
    return jax.shard_map(
        body,
        mesh=mesh,
        in_specs=(
            P(None, "lat", "lon", None),
            P("lat", "lon"),
            P(),
            P("segment", None, None),
            P("segment", None, None),
            P(),
            P(),
        ),
        out_specs=P("segment", None, "lat", "lon", None),
        check_vma=False,
    )
```

```python
import functools
import math

import jax
import jax.numpy as jnp
from jax import lax
from jax.experimental import pallas as pl
from jax.experimental.pallas import tpu as pltpu
from jax.sharding import PartitionSpec as P

HEADS = 16
WLAT = 6
WLON = 12
HALF_LAT = WLAT // 2
HALF_LON = WLON // 2
STEPS = 4
PAIR = 128
NT = (((1,), (1,)), ((), ()))


def based(offset, window):
    return jnp.where(offset >= window // 2, offset - window, offset)


def cell_codes(base, offset, shape, axis, total_rows):
    cell = lax.broadcasted_iota(jnp.int32, shape, axis)
    line = jnp.zeros(shape, jnp.int32)
    for start in range(WLON, shape[axis], WLON):
        line += (cell >= start).astype(jnp.int32)
    block = jnp.zeros(shape, jnp.int32)
    for start in range(WLAT, shape[axis] // WLON, WLAT):
        block += (line >= start).astype(jnp.int32)
    held = base + line - WLAT * block
    held = jnp.where(held < 0, held + total_rows, held)
    held = jnp.where(held >= total_rows, held - total_rows, held)
    return 2 * block + (held < offset).astype(jnp.int32)


def attend_kernel(section, offsets_ref, x_ref, wq_ref, wk_ref, wv_ref, wo_ref, gain_ref, out_ref, total, *, head_size, total_rows):
    step = pl.program_id(0)
    x = x_ref[...]
    q = jnp.dot(x, wq_ref[...], preferred_element_type=jnp.float32).astype(jnp.bfloat16)
    k = jnp.dot(x, wk_ref[...], preferred_element_type=jnp.float32).astype(jnp.bfloat16)
    v = jnp.dot(x, wv_ref[...], preferred_element_type=jnp.float32).astype(jnp.bfloat16)
    cells = x.shape[0]
    offset = offsets_ref[section, 0]
    base = lax.axis_index("lat") * WLAT + based(offset, WLAT)
    allowed = cell_codes(base, offset, (cells, 1), 0, total_rows) == cell_codes(base, offset, (1, cells), 1, total_rows)
    scale = 1.0 / math.sqrt(head_size)
    first_half = lax.broadcasted_iota(jnp.int32, (x.shape[0], PAIR), 1) < head_size
    parts = []
    for pair in range(q.shape[1] // PAIR):
        columns = slice(pair * PAIR, (pair + 1) * PAIR)
        q2, k2, v2 = q[:, columns], k[:, columns], v[:, columns]
        weighted = []
        for keep in (first_half, ~first_half):
            qh = jnp.where(keep, q2, jnp.zeros_like(q2))
            scores = lax.dot_general(qh, k2, NT, preferred_element_type=jnp.float32) * scale
            scores = jnp.where(allowed, scores, -1e30)
            weights = jnp.exp(scores - jnp.max(scores, axis=-1, keepdims=True))
            inverse = 1.0 / jnp.sum(weights, axis=-1, keepdims=True)
            probs = (weights * inverse).astype(jnp.bfloat16)
            weighted.append(jnp.dot(probs, v2, preferred_element_type=jnp.float32))
        parts.append(jnp.where(first_half, weighted[0], weighted[1]).astype(jnp.bfloat16))
    attended = jnp.concatenate(parts, axis=1)
    projected = jnp.dot(attended, wo_ref[...], preferred_element_type=jnp.float32)

    @pl.when(step == 0)
    def _():
        total[...] = projected

    @pl.when(step > 0)
    def _():
        total[...] += projected

    @pl.when(step == STEPS - 1)
    def _():
        whole = total[...]
        gain = jnp.where(lax.axis_index("segment") == 0, gain_ref[0:1, :], gain_ref[1:2, :])
        centered = whole - jnp.mean(whole, axis=-1, keepdims=True)
        variance = jnp.mean(centered * centered, axis=-1, keepdims=True)
        branch = centered * lax.rsqrt(variance + 1e-05) * gain
        out_ref[...] = (x.astype(jnp.float32) + branch).astype(jnp.bfloat16)


def attend(field, section, offsets, wqkv, wout, gain):
    width = field.shape[-1]
    flat = field.reshape(-1, width)
    cells = flat.shape[0]
    slab = width // STEPS
    head_size = width // HEADS
    full = lambda shape: pl.BlockSpec(shape, lambda p: (0, 0))
    return pl.pallas_call(
        functools.partial(
            attend_kernel, section, head_size=head_size, total_rows=WLAT * lax.axis_size("lat")
        ),
        grid=(STEPS,),
        out_shape=jax.ShapeDtypeStruct((cells, width), jnp.bfloat16),
        in_specs=[
            pl.BlockSpec(memory_space=pltpu.SMEM),
            full((cells, width)),
            pl.BlockSpec((width, slab), lambda p: (0, p)),
            pl.BlockSpec((width, slab), lambda p: (0, p + STEPS)),
            pl.BlockSpec((width, slab), lambda p: (0, p + 2 * STEPS)),
            pl.BlockSpec((slab, width), lambda p: (p, 0)),
            full(gain.shape),
        ],
        out_specs=full((cells, width)),
        scratch_shapes=[pltpu.VMEM((cells, width), jnp.float32)],
        compiler_params=pltpu.CompilerParams(vmem_limit_bytes=56 * 1024 * 1024),
        cost_estimate=pl.CostEstimate(
            flops=8 * cells * width * width, bytes_accessed=8 * width * width, transcendentals=HEADS * cells * cells
        ),
    )(offsets, flat, wqkv, wqkv, wqkv, wout, gain)


def exchange_kernel(lat_steps, lon_steps, below_in, corner_in, beside_in, below, corner, beside, send_sem, recv_sem):
    segment, lon, lat = (lax.axis_index(axis) for axis in ("segment", "lon", "lat"))
    lons, lats = lax.axis_size("lon"), lax.axis_size("lat")
    pick = lambda steps: steps[0] + segment * (steps[1] - steps[0])
    lat_step, lon_step = pick(lat_steps), pick(lon_steps)
    place = lambda a, b: (segment, lax.rem(lon + b + lons, lons), lax.rem(lat + a + lats, lats))
    ways = ((lat_step, lon_step), (lat_step, 0), (0, lon_step))
    barrier = pltpu.get_barrier_semaphore()
    for a, b in ways:
        pl.semaphore_signal(barrier, inc=1, device_id=place(a, b), device_id_type=pl.DeviceIdType.MESH)
    pl.semaphore_wait(barrier, 3)
    copies = []
    for index, ((a, b), source, target) in enumerate(
        zip(ways, (corner_in, below_in, beside_in), (corner, below, beside))
    ):
        copy = pltpu.make_async_remote_copy(
            src_ref=source,
            dst_ref=target,
            send_sem=send_sem.at[index],
            recv_sem=recv_sem.at[index],
            device_id=place(-a, -b),
            device_id_type=pl.DeviceIdType.MESH,
        )
        copy.start()
        copies.append(copy)
    for copy in copies:
        copy.wait()


def exchanged(lat_steps, lon_steps, pieces):
    width = pieces[0].shape[-1]
    flats = []
    for piece in pieces:
        flat = piece.reshape(-1, width)
        flats.append(jnp.pad(flat, ((0, -flat.shape[0] % 16), (0, 0))))
    signs = [(1, 1), (1, -1), (-1, 1), (-1, -1)]
    in_vmem = pl.BlockSpec(memory_space=pltpu.VMEM)
    results = pl.pallas_call(
        functools.partial(exchange_kernel, lat_steps, lon_steps),
        out_shape=[jax.ShapeDtypeStruct(flat.shape, flat.dtype) for flat in flats],
        in_specs=[in_vmem] * 3,
        out_specs=[in_vmem] * 3,
        scratch_shapes=[pltpu.SemaphoreType.DMA((3,)), pltpu.SemaphoreType.DMA((3,))],
        compiler_params=pltpu.CompilerParams(
            collective_id=4 * signs.index(lat_steps) + signs.index(lon_steps),
            has_side_effects=True,
            vmem_limit_bytes=8 * 1024 * 1024,
        ),
    )(*flats)
    return [out[: math.prod(piece.shape[:-1])].reshape(piece.shape) for out, piece in zip(results, pieces)]


def by_segment(make, steps):
    if steps[0] == steps[1]:
        return make(steps[0])
    return jnp.where(lax.axis_index("segment") == 0, make(steps[0]), make(steps[1]))


def neighbours(lat_steps, lon_steps, field):
    rows = lambda step: field[:, :HALF_LAT] if step > 0 else field[:, WLAT - HALF_LAT:]
    columns = lambda part: lambda step: part[:, :, :HALF_LON] if step > 0 else part[:, :, WLON - HALF_LON:]
    row_piece = by_segment(rows, lat_steps)
    corner_piece = by_segment(columns(row_piece), lon_steps)
    column_piece = by_segment(columns(field), lon_steps)
    return exchanged(lat_steps, lon_steps, (row_piece, corner_piece, column_piece))


def assembled(field, below, corner, beside, lat_shift, lon_shift):
    near = jnp.concatenate([beside, field, beside], axis=2)
    near = lax.dynamic_slice_in_dim(near, HALF_LON + lon_shift, field.shape[2], 2)
    far = jnp.concatenate([corner, below, corner], axis=2)
    far = lax.dynamic_slice_in_dim(far, HALF_LON + lon_shift, field.shape[2], 2)
    tall = jnp.concatenate([far, near, far], axis=1)
    return lax.dynamic_slice_in_dim(tall, HALF_LAT + lat_shift, field.shape[1], 1)


def sign_of(lat_shift, lon_shift):
    return 2 * (lat_shift < 0).astype(jnp.int32) + (lon_shift < 0).astype(jnp.int32)


def shift(field, lat_shift, lon_shift):
    ways = [functools.partial(neighbours, (a, a), (b, b)) for a in (1, -1) for b in (1, -1)]
    pieces = lax.switch(sign_of(lat_shift, lon_shift), ways, field)
    return assembled(field, *pieces, lat_shift, lon_shift)


def shift_each(field, lat_shifts, lon_shifts):
    signs = [sign_of(*pair) for pair in zip(lat_shifts, lon_shifts)]
    choice = jnp.where(signs[1] > 0, 4 + signs[1], signs[0])
    ways = []
    for segment in (0, 1):
        for a in (1, -1):
            for b in (1, -1):
                lat_steps = (a, 1) if segment == 0 else (1, a)
                lon_steps = (b, 1) if segment == 0 else (1, b)
                ways.append(functools.partial(neighbours, lat_steps, lon_steps))
    pieces = lax.switch(choice, ways, field)
    first = lax.axis_index("segment") == 0
    return assembled(field, *pieces, jnp.where(first, *lat_shifts), jnp.where(first, *lon_shifts))


def body(latents, land_mask, land_embed, qkv_weight, out_weight, norm_gain, offsets):
    segment_index = lax.axis_index("segment")
    assert latents.shape[1:3] == (WLAT, WLON)
    embedded = latents.astype(jnp.float32) + land_embed.astype(jnp.float32)
    seeded = jnp.where(land_mask[None, :, :, None] > 0, embedded, latents.astype(jnp.float32)).astype(jnp.bfloat16)
    wqkv = qkv_weight[0]
    wout = out_weight[0]
    lat_base, lon_base = [], []
    for s in (0, 1):
        lat_base.append(based(offsets[s, 0], WLAT))
        lon_base.append(based(offsets[s, 1], WLON))
    first_in = shift(seeded, lat_base[0], lon_base[0])
    first = attend(first_in, 0, offsets, wqkv, wout, norm_gain)
    passed = lax.ppermute(first, "segment", [(0, 1)]).reshape(latents.shape)
    second_in = shift(passed, lat_base[1] - lat_base[0], lon_base[1] - lon_base[0])
    second = attend(second_in, 1, offsets, wqkv, wout, norm_gain)
    merged = jnp.where(segment_index == 0, first, second).reshape(latents.shape)
    return shift_each(merged, [-x for x in lat_base], [-x for x in lon_base])[None]


def solution(mesh):
    return jax.shard_map(
        body,
        mesh=mesh,
        in_specs=(
            P(None, "lat", "lon", None),
            P("lat", "lon"),
            P(),
            P("segment", None, None),
            P("segment", None, None),
            P(),
            P(),
        ),
        out_specs=P("segment", None, "lat", "lon", None),
        check_vma=False,
    )
```

```python
import functools
import math

import jax
import jax.numpy as jnp
from jax import lax
from jax.experimental import pallas as pl
from jax.experimental.pallas import tpu as pltpu
from jax.sharding import PartitionSpec as P

HEADS = 16
WLAT = 6
WLON = 12
HALF_LAT = WLAT // 2
HALF_LON = WLON // 2
STEPS = 4
PAIR = 128
CHUNK = 48
NT = (((1,), (1,)), ((), ()))


def based(offset, window):
    return jnp.where(offset >= window // 2, offset - window, offset)


def cell_codes(base, offset, shape, axis, total_rows):
    cell = lax.broadcasted_iota(jnp.int32, shape, axis)
    line = jnp.zeros(shape, jnp.int32)
    for start in range(WLON, shape[axis], WLON):
        line += (cell >= start).astype(jnp.int32)
    block = jnp.zeros(shape, jnp.int32)
    for start in range(WLAT, shape[axis] // WLON, WLAT):
        block += (line >= start).astype(jnp.int32)
    held = base + line - WLAT * block
    held = jnp.where(held < 0, held + total_rows, held)
    held = jnp.where(held >= total_rows, held - total_rows, held)
    return 2 * block + (held < offset).astype(jnp.int32)


def attend_kernel(section, offsets_ref, x_ref, wq_ref, wk_ref, wv_ref, wo_ref, gain_ref, out_ref, *rest, head_size, total_rows, hop):
    if hop:
        passed_ref, total, staged, send_sem, recv_sem, local_sem = rest
    else:
        (total,) = rest
    step = pl.program_id(0)
    segment, lon, lat = (lax.axis_index(axis) for axis in ("segment", "lon", "lat"))
    if hop:
        barrier = pltpu.get_barrier_semaphore()
        partner = (1 - segment, lon, lat)

        @pl.when((step == 0) & (segment == 1))
        def _():
            pl.semaphore_signal(barrier, inc=1, device_id=partner, device_id_type=pl.DeviceIdType.MESH)

        def hop_copy(index):
            rows = pl.ds(index * CHUNK, CHUNK)
            return pltpu.make_async_remote_copy(
                src_ref=staged.at[rows],
                dst_ref=passed_ref.at[rows],
                send_sem=send_sem.at[index],
                recv_sem=recv_sem.at[index],
                device_id=partner,
                device_id_type=pl.DeviceIdType.MESH,
            )

    x = x_ref[...]
    q = jnp.dot(x, wq_ref[...], preferred_element_type=jnp.float32).astype(jnp.bfloat16)
    k = jnp.dot(x, wk_ref[...], preferred_element_type=jnp.float32).astype(jnp.bfloat16)
    v = jnp.dot(x, wv_ref[...], preferred_element_type=jnp.float32).astype(jnp.bfloat16)
    cells = x.shape[0]
    offset = offsets_ref[section, 0]
    base = lat * WLAT + based(offset, WLAT)
    allowed = cell_codes(base, offset, (cells, 1), 0, total_rows) == cell_codes(base, offset, (1, cells), 1, total_rows)
    scale = 1.0 / math.sqrt(head_size)
    first_half = lax.broadcasted_iota(jnp.int32, (x.shape[0], PAIR), 1) < head_size
    parts = []
    for pair in range(q.shape[1] // PAIR):
        columns = slice(pair * PAIR, (pair + 1) * PAIR)
        q2, k2, v2 = q[:, columns], k[:, columns], v[:, columns]
        weighted = []
        for keep in (first_half, ~first_half):
            qh = jnp.where(keep, q2, jnp.zeros_like(q2))
            scores = lax.dot_general(qh, k2, NT, preferred_element_type=jnp.float32) * scale
            scores = jnp.where(allowed, scores, -1e30)
            weights = jnp.exp(scores - jnp.max(scores, axis=-1, keepdims=True))
            inverse = 1.0 / jnp.sum(weights, axis=-1, keepdims=True)
            probs = (weights * inverse).astype(jnp.bfloat16)
            weighted.append(jnp.dot(probs, v2, preferred_element_type=jnp.float32))
        parts.append(jnp.where(first_half, weighted[0], weighted[1]).astype(jnp.bfloat16))
    attended = jnp.concatenate(parts, axis=1)
    projected = jnp.dot(attended, wo_ref[...], preferred_element_type=jnp.float32)

    @pl.when(step == 0)
    def _():
        total[...] = projected

    @pl.when(step > 0)
    def _():
        total[...] += projected

    @pl.when(step == STEPS - 1)
    def _():
        if hop:

            @pl.when(segment == 0)
            def _():
                pl.semaphore_wait(barrier, 1)

        gain = jnp.where(segment == 0, gain_ref[0:1, :], gain_ref[1:2, :])
        chunks = cells // CHUNK
        for index in range(chunks):
            rows = pl.ds(index * CHUNK, CHUNK)
            whole = total[rows, :]
            centered = whole - jnp.mean(whole, axis=-1, keepdims=True)
            variance = jnp.mean(centered * centered, axis=-1, keepdims=True)
            branch = centered * lax.rsqrt(variance + 1e-05) * gain
            summed = (x_ref[rows, :].astype(jnp.float32) + branch).astype(jnp.bfloat16)
            out_ref[rows, :] = summed
            if hop:
                staged[rows, :] = summed

                @pl.when(segment == 0)
                def _():
                    hop_copy(index).start()

        if hop:

            @pl.when(segment == 0)
            def _():
                kept = pltpu.make_async_copy(staged, passed_ref, local_sem)
                kept.start()
                for index in range(chunks):
                    hop_copy(index).wait_send()
                kept.wait()

            @pl.when(segment == 1)
            def _():
                for index in range(chunks):
                    hop_copy(index).wait_recv()


def attend(field, section, offsets, wqkv, wout, gain):
    hop = section == 0
    width = field.shape[-1]
    flat = field.reshape(-1, width)
    cells = flat.shape[0]
    assert cells % CHUNK == 0
    slab = width // STEPS
    head_size = width // HEADS
    hop_scratch = [
        pltpu.VMEM((cells, width), jnp.bfloat16),
        pltpu.SemaphoreType.DMA((cells // CHUNK,)),
        pltpu.SemaphoreType.DMA((cells // CHUNK,)),
        pltpu.SemaphoreType.DMA,
    ]
    full = lambda shape: pl.BlockSpec(shape, lambda p: (0, 0))
    return pl.pallas_call(
        functools.partial(
            attend_kernel, section, head_size=head_size, total_rows=WLAT * lax.axis_size("lat"), hop=hop
        ),
        grid=(STEPS,),
        out_shape=[jax.ShapeDtypeStruct((cells, width), jnp.bfloat16)] * (2 if hop else 1),
        in_specs=[
            pl.BlockSpec(memory_space=pltpu.SMEM),
            full((cells, width)),
            pl.BlockSpec((width, slab), lambda p: (0, p)),
            pl.BlockSpec((width, slab), lambda p: (0, p + STEPS)),
            pl.BlockSpec((width, slab), lambda p: (0, p + 2 * STEPS)),
            pl.BlockSpec((slab, width), lambda p: (p, 0)),
            full(gain.shape),
        ],
        out_specs=[full((cells, width))] + ([pl.BlockSpec(memory_space=pl.ANY)] if hop else []),
        scratch_shapes=[pltpu.VMEM((cells, width), jnp.float32)] + (hop_scratch if hop else []),
        compiler_params=pltpu.CompilerParams(
            vmem_limit_bytes=56 * 1024 * 1024,
            collective_id=16 if hop else None,
            has_side_effects=hop,
        ),
        cost_estimate=pl.CostEstimate(
            flops=8 * cells * width * width, bytes_accessed=8 * width * width, transcendentals=HEADS * cells * cells
        ),
    )(offsets, flat, wqkv, wqkv, wqkv, wout, gain)


def exchange_kernel(lat_steps, lon_steps, below_in, corner_in, beside_in, below, corner, beside, send_sem, recv_sem):
    segment, lon, lat = (lax.axis_index(axis) for axis in ("segment", "lon", "lat"))
    lons, lats = lax.axis_size("lon"), lax.axis_size("lat")
    pick = lambda steps: steps[0] + segment * (steps[1] - steps[0])
    lat_step, lon_step = pick(lat_steps), pick(lon_steps)
    place = lambda a, b: (segment, lax.rem(lon + b + lons, lons), lax.rem(lat + a + lats, lats))
    ways = ((lat_step, lon_step), (lat_step, 0), (0, lon_step))
    barrier = pltpu.get_barrier_semaphore()
    for a, b in ways:
        pl.semaphore_signal(barrier, inc=1, device_id=place(a, b), device_id_type=pl.DeviceIdType.MESH)
    pl.semaphore_wait(barrier, 3)
    copies = []
    for index, ((a, b), source, target) in enumerate(
        zip(ways, (corner_in, below_in, beside_in), (corner, below, beside))
    ):
        copy = pltpu.make_async_remote_copy(
            src_ref=source,
            dst_ref=target,
            send_sem=send_sem.at[index],
            recv_sem=recv_sem.at[index],
            device_id=place(-a, -b),
            device_id_type=pl.DeviceIdType.MESH,
        )
        copy.start()
        copies.append(copy)
    for copy in copies:
        copy.wait()


def exchanged(lat_steps, lon_steps, pieces):
    width = pieces[0].shape[-1]
    flats = []
    for piece in pieces:
        flat = piece.reshape(-1, width)
        flats.append(jnp.pad(flat, ((0, -flat.shape[0] % 16), (0, 0))))
    signs = [(1, 1), (1, -1), (-1, 1), (-1, -1)]
    in_vmem = pl.BlockSpec(memory_space=pltpu.VMEM)
    results = pl.pallas_call(
        functools.partial(exchange_kernel, lat_steps, lon_steps),
        out_shape=[jax.ShapeDtypeStruct(flat.shape, flat.dtype) for flat in flats],
        in_specs=[in_vmem] * 3,
        out_specs=[in_vmem] * 3,
        scratch_shapes=[pltpu.SemaphoreType.DMA((3,)), pltpu.SemaphoreType.DMA((3,))],
        compiler_params=pltpu.CompilerParams(
            collective_id=4 * signs.index(lat_steps) + signs.index(lon_steps),
            has_side_effects=True,
            vmem_limit_bytes=8 * 1024 * 1024,
        ),
    )(*flats)
    return [out[: math.prod(piece.shape[:-1])].reshape(piece.shape) for out, piece in zip(results, pieces)]


def by_segment(make, steps):
    if steps[0] == steps[1]:
        return make(steps[0])
    return jnp.where(lax.axis_index("segment") == 0, make(steps[0]), make(steps[1]))


def neighbours(lat_steps, lon_steps, field):
    rows = lambda step: field[:, :HALF_LAT] if step > 0 else field[:, WLAT - HALF_LAT:]
    columns = lambda part: lambda step: part[:, :, :HALF_LON] if step > 0 else part[:, :, WLON - HALF_LON:]
    row_piece = by_segment(rows, lat_steps)
    corner_piece = by_segment(columns(row_piece), lon_steps)
    column_piece = by_segment(columns(field), lon_steps)
    return exchanged(lat_steps, lon_steps, (row_piece, corner_piece, column_piece))


def assembled(field, below, corner, beside, lat_shift, lon_shift):
    near = jnp.concatenate([beside, field, beside], axis=2)
    near = lax.dynamic_slice_in_dim(near, HALF_LON + lon_shift, field.shape[2], 2)
    far = jnp.concatenate([corner, below, corner], axis=2)
    far = lax.dynamic_slice_in_dim(far, HALF_LON + lon_shift, field.shape[2], 2)
    tall = jnp.concatenate([far, near, far], axis=1)
    return lax.dynamic_slice_in_dim(tall, HALF_LAT + lat_shift, field.shape[1], 1)


def sign_of(lat_shift, lon_shift):
    return 2 * (lat_shift < 0).astype(jnp.int32) + (lon_shift < 0).astype(jnp.int32)


def shift(field, lat_shift, lon_shift):
    ways = [functools.partial(neighbours, (a, a), (b, b)) for a in (1, -1) for b in (1, -1)]
    pieces = lax.switch(sign_of(lat_shift, lon_shift), ways, field)
    return assembled(field, *pieces, lat_shift, lon_shift)


def shift_each(field, lat_shifts, lon_shifts):
    signs = [sign_of(*pair) for pair in zip(lat_shifts, lon_shifts)]
    choice = jnp.where(signs[1] > 0, 4 + signs[1], signs[0])
    ways = []
    for segment in (0, 1):
        for a in (1, -1):
            for b in (1, -1):
                lat_steps = (a, 1) if segment == 0 else (1, a)
                lon_steps = (b, 1) if segment == 0 else (1, b)
                ways.append(functools.partial(neighbours, lat_steps, lon_steps))
    pieces = lax.switch(choice, ways, field)
    first = lax.axis_index("segment") == 0
    return assembled(field, *pieces, jnp.where(first, *lat_shifts), jnp.where(first, *lon_shifts))


def body(latents, land_mask, land_embed, qkv_weight, out_weight, norm_gain, offsets):
    segment_index = lax.axis_index("segment")
    assert latents.shape[1:3] == (WLAT, WLON)
    embedded = latents.astype(jnp.float32) + land_embed.astype(jnp.float32)
    seeded = jnp.where(land_mask[None, :, :, None] > 0, embedded, latents.astype(jnp.float32)).astype(jnp.bfloat16)
    wqkv = qkv_weight[0]
    wout = out_weight[0]
    lat_base, lon_base = [], []
    for s in (0, 1):
        lat_base.append(based(offsets[s, 0], WLAT))
        lon_base.append(based(offsets[s, 1], WLON))
    first_in = shift(seeded, lat_base[0], lon_base[0])
    first, passed = attend(first_in, 0, offsets, wqkv, wout, norm_gain)
    passed = passed.reshape(latents.shape)
    second_in = shift(passed, lat_base[1] - lat_base[0], lon_base[1] - lon_base[0])
    (second,) = attend(second_in, 1, offsets, wqkv, wout, norm_gain)
    merged = jnp.where(segment_index == 0, first, second).reshape(latents.shape)
    return shift_each(merged, [-x for x in lat_base], [-x for x in lon_base])[None]


def solution(mesh):
    return jax.shard_map(
        body,
        mesh=mesh,
        in_specs=(
            P(None, "lat", "lon", None),
            P("lat", "lon"),
            P(),
            P("segment", None, None),
            P("segment", None, None),
            P(),
            P(),
        ),
        out_specs=P("segment", None, "lat", "lon", None),
        check_vma=False,
    )
```

```python
import functools
import math

import jax
import jax.numpy as jnp
from jax import lax
from jax.experimental import pallas as pl
from jax.experimental.pallas import tpu as pltpu
from jax.sharding import PartitionSpec as P

HEADS = 16
WLAT = 6
WLON = 12
HALF_LAT = WLAT // 2
HALF_LON = WLON // 2
STEPS = 4
PAIR = 128
CHUNK = 48
NT = (((1,), (1,)), ((), ()))


def based(offset, window):
    return jnp.where(offset >= window // 2, offset - window, offset)


def cell_codes(base, offset, shape, axis, total_rows):
    cell = lax.broadcasted_iota(jnp.int32, shape, axis)
    line = jnp.zeros(shape, jnp.int32)
    for start in range(WLON, shape[axis], WLON):
        line += (cell >= start).astype(jnp.int32)
    block = jnp.zeros(shape, jnp.int32)
    for start in range(WLAT, shape[axis] // WLON, WLAT):
        block += (line >= start).astype(jnp.int32)
    held = base + line - WLAT * block
    held = jnp.where(held < 0, held + total_rows, held)
    held = jnp.where(held >= total_rows, held - total_rows, held)
    return 2 * block + (held < offset).astype(jnp.int32)


def attend_kernel(section, offsets_ref, x_ref, wq_ref, wk_ref, wv_ref, wo_ref, gain_ref, out_ref, *rest, head_size, total_rows, hop):
    if hop:
        passed_ref, total, staged, send_sem, recv_sem, local_sem = rest
    else:
        (total,) = rest
    step = pl.program_id(0)
    segment, lon, lat = (lax.axis_index(axis) for axis in ("segment", "lon", "lat"))
    if hop:
        barrier = pltpu.get_barrier_semaphore()
        partner = (1 - segment, lon, lat)

        @pl.when((step == 0) & (segment == 1))
        def _():
            pl.semaphore_signal(barrier, inc=1, device_id=partner, device_id_type=pl.DeviceIdType.MESH)

        def hop_copy(index):
            rows = pl.ds(index * CHUNK, CHUNK)
            return pltpu.make_async_remote_copy(
                src_ref=staged.at[rows],
                dst_ref=passed_ref.at[rows],
                send_sem=send_sem.at[index],
                recv_sem=recv_sem.at[index],
                device_id=partner,
                device_id_type=pl.DeviceIdType.MESH,
            )

    x = x_ref[...]
    q = jnp.dot(x, wq_ref[...], preferred_element_type=jnp.float32).astype(jnp.bfloat16)
    k = jnp.dot(x, wk_ref[...], preferred_element_type=jnp.float32).astype(jnp.bfloat16)
    v = jnp.dot(x, wv_ref[...], preferred_element_type=jnp.float32).astype(jnp.bfloat16)
    cells = x.shape[0]
    offset = offsets_ref[section, 0]
    base = lat * WLAT + based(offset, WLAT)
    allowed = cell_codes(base, offset, (cells, 1), 0, total_rows) == cell_codes(base, offset, (1, cells), 1, total_rows)
    scale = 1.0 / math.sqrt(head_size)
    first_half = lax.broadcasted_iota(jnp.int32, (x.shape[0], PAIR), 1) < head_size
    parts = []
    for pair in range(q.shape[1] // PAIR):
        columns = slice(pair * PAIR, (pair + 1) * PAIR)
        q2, k2, v2 = q[:, columns], k[:, columns], v[:, columns]
        weighted = []
        for keep in (first_half, ~first_half):
            qh = jnp.where(keep, q2, jnp.zeros_like(q2))
            scores = lax.dot_general(qh, k2, NT, preferred_element_type=jnp.float32) * scale
            scores = jnp.where(allowed, scores, -1e30)
            weights = jnp.exp(scores - jnp.max(scores, axis=-1, keepdims=True))
            inverse = 1.0 / jnp.sum(weights, axis=-1, keepdims=True)
            probs = (weights * inverse).astype(jnp.bfloat16)
            weighted.append(jnp.dot(probs, v2, preferred_element_type=jnp.float32))
        parts.append(jnp.where(first_half, weighted[0], weighted[1]).astype(jnp.bfloat16))
    attended = jnp.concatenate(parts, axis=1)
    projected = jnp.dot(attended, wo_ref[...], preferred_element_type=jnp.float32)

    @pl.when(step == 0)
    def _():
        total[...] = projected

    @pl.when(step > 0)
    def _():
        total[...] += projected

    @pl.when(step == STEPS - 1)
    def _():
        if hop:

            @pl.when(segment == 0)
            def _():
                pl.semaphore_wait(barrier, 1)

        gain = jnp.where(segment == 0, gain_ref[0:1, :], gain_ref[1:2, :])
        chunks = cells // CHUNK
        for index in range(chunks):
            rows = pl.ds(index * CHUNK, CHUNK)
            whole = total[rows, :]
            centered = whole - jnp.mean(whole, axis=-1, keepdims=True)
            variance = jnp.mean(centered * centered, axis=-1, keepdims=True)
            branch = centered * lax.rsqrt(variance + 1e-05) * gain
            summed = (x_ref[rows, :].astype(jnp.float32) + branch).astype(jnp.bfloat16)
            out_ref[rows, :] = summed
            if hop:
                staged[rows, :] = summed

                @pl.when(segment == 0)
                def _():
                    hop_copy(index).start()

        if hop:

            @pl.when(segment == 0)
            def _():
                kept = pltpu.make_async_copy(staged, passed_ref, local_sem)
                kept.start()
                for index in range(chunks):
                    hop_copy(index).wait_send()
                kept.wait()

            @pl.when(segment == 1)
            def _():
                for index in range(chunks):
                    hop_copy(index).wait_recv()


def attend(field, section, offsets, wqkv, wout, gain):
    hop = section == 0
    width = field.shape[-1]
    flat = field.reshape(-1, width)
    cells = flat.shape[0]
    assert cells % CHUNK == 0
    slab = width // STEPS
    head_size = width // HEADS
    hop_scratch = [
        pltpu.VMEM((cells, width), jnp.bfloat16),
        pltpu.SemaphoreType.DMA((cells // CHUNK,)),
        pltpu.SemaphoreType.DMA((cells // CHUNK,)),
        pltpu.SemaphoreType.DMA,
    ]
    full = lambda shape: pl.BlockSpec(shape, lambda p: (0, 0))
    return pl.pallas_call(
        functools.partial(
            attend_kernel, section, head_size=head_size, total_rows=WLAT * lax.axis_size("lat"), hop=hop
        ),
        grid=(STEPS,),
        out_shape=[jax.ShapeDtypeStruct((cells, width), jnp.bfloat16)] * (2 if hop else 1),
        in_specs=[
            pl.BlockSpec(memory_space=pltpu.SMEM),
            full((cells, width)),
            pl.BlockSpec((width, slab), lambda p: (0, p)),
            pl.BlockSpec((width, slab), lambda p: (0, p + STEPS)),
            pl.BlockSpec((width, slab), lambda p: (0, p + 2 * STEPS)),
            pl.BlockSpec((slab, width), lambda p: (p, 0)),
            full(gain.shape),
        ],
        out_specs=[full((cells, width))] + ([pl.BlockSpec(memory_space=pl.ANY)] if hop else []),
        scratch_shapes=[pltpu.VMEM((cells, width), jnp.float32)] + (hop_scratch if hop else []),
        compiler_params=pltpu.CompilerParams(
            vmem_limit_bytes=56 * 1024 * 1024,
            collective_id=16 if hop else None,
            has_side_effects=hop,
        ),
        cost_estimate=pl.CostEstimate(
            flops=8 * cells * width * width, bytes_accessed=8 * width * width, transcendentals=HEADS * cells * cells
        ),
    )(offsets, flat, wqkv, wqkv, wqkv, wout, gain)


def exchange_kernel(lat_steps, lon_steps, below_in, corner_in, beside_in, below, corner, beside, send_sem, recv_sem):
    segment, lon, lat = (lax.axis_index(axis) for axis in ("segment", "lon", "lat"))
    lons, lats = lax.axis_size("lon"), lax.axis_size("lat")
    pick = lambda steps: steps[0] + segment * (steps[1] - steps[0])
    lat_step, lon_step = pick(lat_steps), pick(lon_steps)
    place = lambda a, b: (segment, lax.rem(lon + b + lons, lons), lax.rem(lat + a + lats, lats))
    ways = ((lat_step, lon_step), (lat_step, 0), (0, lon_step))
    barrier = pltpu.get_barrier_semaphore()
    for a, b in ways:
        pl.semaphore_signal(barrier, inc=1, device_id=place(a, b), device_id_type=pl.DeviceIdType.MESH)
    pl.semaphore_wait(barrier, 3)
    copies = []
    for index, ((a, b), source, target) in enumerate(
        zip(ways, (corner_in, below_in, beside_in), (corner, below, beside))
    ):
        copy = pltpu.make_async_remote_copy(
            src_ref=source,
            dst_ref=target,
            send_sem=send_sem.at[index],
            recv_sem=recv_sem.at[index],
            device_id=place(-a, -b),
            device_id_type=pl.DeviceIdType.MESH,
        )
        copy.start()
        copies.append(copy)
    for copy in copies:
        copy.wait()


def exchanged(lat_steps, lon_steps, pieces):
    width = pieces[0].shape[-1]
    flats = []
    for piece in pieces:
        flat = piece.reshape(-1, width)
        flats.append(jnp.pad(flat, ((0, -flat.shape[0] % 16), (0, 0))))
    signs = [(1, 1), (1, -1), (-1, 1), (-1, -1)]
    in_vmem = pl.BlockSpec(memory_space=pltpu.VMEM)
    results = pl.pallas_call(
        functools.partial(exchange_kernel, lat_steps, lon_steps),
        out_shape=[jax.ShapeDtypeStruct(flat.shape, flat.dtype) for flat in flats],
        in_specs=[in_vmem] * 3,
        out_specs=[in_vmem] * 3,
        scratch_shapes=[pltpu.SemaphoreType.DMA((3,)), pltpu.SemaphoreType.DMA((3,))],
        compiler_params=pltpu.CompilerParams(
            collective_id=4 * signs.index(lat_steps) + signs.index(lon_steps),
            has_side_effects=True,
            vmem_limit_bytes=8 * 1024 * 1024,
        ),
    )(*flats)
    return [out[: math.prod(piece.shape[:-1])].reshape(piece.shape) for out, piece in zip(results, pieces)]


def by_segment(make, steps):
    if steps[0] == steps[1]:
        return make(steps[0])
    return jnp.where(lax.axis_index("segment") == 0, make(steps[0]), make(steps[1]))


def neighbours(lat_steps, lon_steps, field):
    rows = lambda step: field[:, :HALF_LAT] if step > 0 else field[:, WLAT - HALF_LAT:]
    columns = lambda part: lambda step: part[:, :, :HALF_LON] if step > 0 else part[:, :, WLON - HALF_LON:]
    row_piece = by_segment(rows, lat_steps)
    corner_piece = by_segment(columns(row_piece), lon_steps)
    column_piece = by_segment(columns(field), lon_steps)
    return exchanged(lat_steps, lon_steps, (row_piece, corner_piece, column_piece))


def assembled(field, below, corner, beside, row, column):
    sliced = functools.partial(lax.dynamic_slice_in_dim, allow_negative_indices=False)
    near = jnp.concatenate([beside, field, beside], axis=2)
    near = sliced(near, column, field.shape[2], 2)
    far = jnp.concatenate([corner, below, corner], axis=2)
    far = sliced(far, column, field.shape[2], 2)
    tall = jnp.concatenate([far, near, far], axis=1)
    return sliced(tall, row, field.shape[1], 1)


def sign_of(lat_shift, lon_shift):
    return jnp.where(lat_shift < 0, 2, 0) + jnp.where(lon_shift < 0, 1, 0)


def plan_kernel(offsets_ref, *outs):
    lat_base = [based(offsets_ref[s, 0], WLAT) for s in (0, 1)]
    lon_base = [based(offsets_ref[s, 1], WLON) for s in (0, 1)]
    first = lax.axis_index("segment") == 0
    lat_step, lon_step = lat_base[1] - lat_base[0], lon_base[1] - lon_base[0]
    back = [sign_of(-lat_base[s], -lon_base[s]) for s in (0, 1)]
    numbers = (
        sign_of(lat_base[0], lon_base[0]),
        HALF_LAT + lat_base[0],
        HALF_LON + lon_base[0],
        sign_of(lat_step, lon_step),
        HALF_LAT + lat_step,
        HALF_LON + lon_step,
        jnp.where(back[1] > 0, 4 + back[1], back[0]),
        HALF_LAT - jnp.where(first, lat_base[0], lat_base[1]),
        HALF_LON - jnp.where(first, lon_base[0], lon_base[1]),
    )
    for out, number in zip(outs, numbers):
        out[0] = number


def planned(offsets):
    in_smem = pl.BlockSpec(memory_space=pltpu.SMEM)
    numbers = pl.pallas_call(
        plan_kernel,
        out_shape=[jax.ShapeDtypeStruct((1,), jnp.int32)] * 9,
        in_specs=[in_smem],
        out_specs=[in_smem] * 9,
    )(offsets)
    numbers = [number.reshape(()) for number in numbers]
    return numbers[:3], numbers[3:6], numbers[6:]


def shift(field, choice, row, column):
    ways = [functools.partial(neighbours, (a, a), (b, b)) for a in (1, -1) for b in (1, -1)]
    return assembled(field, *lax.switch(choice, ways, field), row, column)


def shift_each(field, choice, row, column):
    ways = []
    for segment in (0, 1):
        for a in (1, -1):
            for b in (1, -1):
                lat_steps = (a, 1) if segment == 0 else (1, a)
                lon_steps = (b, 1) if segment == 0 else (1, b)
                ways.append(functools.partial(neighbours, lat_steps, lon_steps))
    return assembled(field, *lax.switch(choice, ways, field), row, column)


def body(latents, land_mask, land_embed, qkv_weight, out_weight, norm_gain, offsets):
    segment_index = lax.axis_index("segment")
    assert latents.shape[1:3] == (WLAT, WLON)
    embedded = latents.astype(jnp.float32) + land_embed.astype(jnp.float32)
    seeded = jnp.where(land_mask[None, :, :, None] > 0, embedded, latents.astype(jnp.float32)).astype(jnp.bfloat16)
    wqkv = qkv_weight[0]
    wout = out_weight[0]
    into_first, into_second, back = planned(offsets)
    first_in = shift(seeded, *into_first)
    first, passed = attend(first_in, 0, offsets, wqkv, wout, norm_gain)
    passed = passed.reshape(latents.shape)
    second_in = shift(passed, *into_second)
    (second,) = attend(second_in, 1, offsets, wqkv, wout, norm_gain)
    merged = jnp.where(segment_index == 0, first, second).reshape(latents.shape)
    return shift_each(merged, *back)[None]


def solution(mesh):
    return jax.shard_map(
        body,
        mesh=mesh,
        in_specs=(
            P(None, "lat", "lon", None),
            P("lat", "lon"),
            P(),
            P("segment", None, None),
            P("segment", None, None),
            P(),
            P(),
        ),
        out_specs=P("segment", None, "lat", "lon", None),
        check_vma=False,
    )
```

```python
import functools
import math

import jax
import jax.numpy as jnp
from jax import lax
from jax.experimental import pallas as pl
from jax.experimental.pallas import tpu as pltpu
from jax.sharding import PartitionSpec as P

HEADS = 16
WLAT = 6
WLON = 12
HALF_LAT = WLAT // 2
HALF_LON = WLON // 2
STEPS = 4
PAIR = 128
CHUNK = 48
NT = (((1,), (1,)), ((), ()))


def based(offset, window):
    return jnp.where(offset >= window // 2, offset - window, offset)


def cell_codes(base, offset, shape, axis, total_rows):
    cell = lax.broadcasted_iota(jnp.int32, shape, axis)
    line = jnp.zeros(shape, jnp.int32)
    for start in range(WLON, shape[axis], WLON):
        line += (cell >= start).astype(jnp.int32)
    block = jnp.zeros(shape, jnp.int32)
    for start in range(WLAT, shape[axis] // WLON, WLAT):
        block += (line >= start).astype(jnp.int32)
    held = base + line - WLAT * block
    held = jnp.where(held < 0, held + total_rows, held)
    held = jnp.where(held >= total_rows, held - total_rows, held)
    return 2 * block + (held < offset).astype(jnp.int32)


def attend_kernel(section, offsets_ref, x_ref, wq_ref, wk_ref, wv_ref, wo_ref, gain_ref, out_ref, *rest, head_size, total_rows, hop):
    if hop:
        passed_ref, total, staged, send_sem, recv_sem, local_sem = rest
    else:
        (total,) = rest
    step = pl.program_id(0)
    segment, lon, lat = (lax.axis_index(axis) for axis in ("segment", "lon", "lat"))
    if hop:
        barrier = pltpu.get_barrier_semaphore()
        partner = (1 - segment, lon, lat)

        @pl.when((step == 0) & (segment == 1))
        def _():
            pl.semaphore_signal(barrier, inc=1, device_id=partner, device_id_type=pl.DeviceIdType.MESH)

        def hop_copy(index):
            rows = pl.ds(index * CHUNK, CHUNK)
            return pltpu.make_async_remote_copy(
                src_ref=staged.at[rows],
                dst_ref=passed_ref.at[rows],
                send_sem=send_sem.at[index],
                recv_sem=recv_sem.at[index],
                device_id=partner,
                device_id_type=pl.DeviceIdType.MESH,
            )

    x = x_ref[...]
    q = jnp.dot(x, wq_ref[...], preferred_element_type=jnp.float32).astype(jnp.bfloat16)
    k = jnp.dot(x, wk_ref[...], preferred_element_type=jnp.float32).astype(jnp.bfloat16)
    v = jnp.dot(x, wv_ref[...], preferred_element_type=jnp.float32).astype(jnp.bfloat16)
    cells = x.shape[0]
    offset = offsets_ref[section, 0]
    base = lat * WLAT + based(offset, WLAT)
    allowed = cell_codes(base, offset, (cells, 1), 0, total_rows) == cell_codes(base, offset, (1, cells), 1, total_rows)
    scale = 1.0 / math.sqrt(head_size)
    first_half = lax.broadcasted_iota(jnp.int32, (x.shape[0], PAIR), 1) < head_size
    parts = []
    for pair in range(q.shape[1] // PAIR):
        columns = slice(pair * PAIR, (pair + 1) * PAIR)
        q2, k2, v2 = q[:, columns], k[:, columns], v[:, columns]
        weighted = []
        for keep in (first_half, ~first_half):
            qh = jnp.where(keep, q2, jnp.zeros_like(q2))
            scores = lax.dot_general(qh, k2, NT, preferred_element_type=jnp.float32) * scale
            scores = jnp.where(allowed, scores, -1e30)
            weights = jnp.exp(scores - jnp.max(scores, axis=-1, keepdims=True))
            inverse = 1.0 / jnp.sum(weights, axis=-1, keepdims=True)
            probs = (weights * inverse).astype(jnp.bfloat16)
            weighted.append(jnp.dot(probs, v2, preferred_element_type=jnp.float32))
        parts.append(jnp.where(first_half, weighted[0], weighted[1]).astype(jnp.bfloat16))
    attended = jnp.concatenate(parts, axis=1)
    projected = jnp.dot(attended, wo_ref[...], preferred_element_type=jnp.float32)

    @pl.when(step == 0)
    def _():
        total[...] = projected

    @pl.when(step > 0)
    def _():
        total[...] += projected

    @pl.when(step == STEPS - 1)
    def _():
        if hop:

            @pl.when(segment == 0)
            def _():
                pl.semaphore_wait(barrier, 1)

        gain = jnp.where(segment == 0, gain_ref[0:1, :], gain_ref[1:2, :])
        chunks = cells // CHUNK
        for index in range(chunks):
            rows = pl.ds(index * CHUNK, CHUNK)
            whole = total[rows, :]
            centered = whole - jnp.mean(whole, axis=-1, keepdims=True)
            variance = jnp.mean(centered * centered, axis=-1, keepdims=True)
            branch = centered * lax.rsqrt(variance + 1e-05) * gain
            summed = (x_ref[rows, :].astype(jnp.float32) + branch).astype(jnp.bfloat16)
            out_ref[rows, :] = summed
            if hop:
                staged[rows, :] = summed

                @pl.when(segment == 0)
                def _():
                    hop_copy(index).start()

        if hop:

            @pl.when(segment == 0)
            def _():
                kept = pltpu.make_async_copy(staged, passed_ref, local_sem)
                kept.start()
                for index in range(chunks):
                    hop_copy(index).wait_send()
                kept.wait()

            @pl.when(segment == 1)
            def _():
                for index in range(chunks):
                    hop_copy(index).wait_recv()


def attend(field, section, offsets, wqkv, wout, gain):
    hop = section == 0
    width = field.shape[-1]
    flat = field.reshape(-1, width)
    cells = flat.shape[0]
    assert cells % CHUNK == 0
    slab = width // STEPS
    head_size = width // HEADS
    hop_scratch = [
        pltpu.VMEM((cells, width), jnp.bfloat16),
        pltpu.SemaphoreType.DMA((cells // CHUNK,)),
        pltpu.SemaphoreType.DMA((cells // CHUNK,)),
        pltpu.SemaphoreType.DMA,
    ]
    full = lambda shape: pl.BlockSpec(shape, lambda p: (0, 0))
    return pl.pallas_call(
        functools.partial(
            attend_kernel, section, head_size=head_size, total_rows=WLAT * lax.axis_size("lat"), hop=hop
        ),
        grid=(STEPS,),
        out_shape=[jax.ShapeDtypeStruct((cells, width), jnp.bfloat16)] * (2 if hop else 1),
        in_specs=[
            pl.BlockSpec(memory_space=pltpu.SMEM),
            full((cells, width)),
            pl.BlockSpec((width, slab), lambda p: (0, p)),
            pl.BlockSpec((width, slab), lambda p: (0, p + STEPS)),
            pl.BlockSpec((width, slab), lambda p: (0, p + 2 * STEPS)),
            pl.BlockSpec((slab, width), lambda p: (p, 0)),
            full(gain.shape),
        ],
        out_specs=[full((cells, width))] + ([pl.BlockSpec(memory_space=pl.ANY)] if hop else []),
        scratch_shapes=[pltpu.VMEM((cells, width), jnp.float32)] + (hop_scratch if hop else []),
        compiler_params=pltpu.CompilerParams(
            vmem_limit_bytes=56 * 1024 * 1024,
            collective_id=16 if hop else None,
            has_side_effects=hop,
        ),
        cost_estimate=pl.CostEstimate(
            flops=8 * cells * width * width, bytes_accessed=8 * width * width, transcendentals=HEADS * cells * cells
        ),
    )(offsets, flat, wqkv, wqkv, wqkv, wout, gain)


def exchange_kernel(lat_steps, lon_steps, below_in, corner_in, beside_in, below, corner, beside, send_sem, recv_sem):
    segment, lon, lat = (lax.axis_index(axis) for axis in ("segment", "lon", "lat"))
    lons, lats = lax.axis_size("lon"), lax.axis_size("lat")
    pick = lambda steps: steps[0] + segment * (steps[1] - steps[0])
    lat_step, lon_step = pick(lat_steps), pick(lon_steps)
    place = lambda a, b: (segment, lax.rem(lon + b + lons, lons), lax.rem(lat + a + lats, lats))
    ways = ((lat_step, lon_step), (lat_step, 0), (0, lon_step))
    barrier = pltpu.get_barrier_semaphore()
    for a, b in ways:
        pl.semaphore_signal(barrier, inc=1, device_id=place(a, b), device_id_type=pl.DeviceIdType.MESH)
    pl.semaphore_wait(barrier, 3)
    copies = []
    for index, ((a, b), source, target) in enumerate(
        zip(ways, (corner_in, below_in, beside_in), (corner, below, beside))
    ):
        copy = pltpu.make_async_remote_copy(
            src_ref=source,
            dst_ref=target,
            send_sem=send_sem.at[index],
            recv_sem=recv_sem.at[index],
            device_id=place(-a, -b),
            device_id_type=pl.DeviceIdType.MESH,
        )
        copy.start()
        copies.append(copy)
    for copy in copies:
        copy.wait()


def exchanged(lat_steps, lon_steps, pieces):
    width = pieces[0].shape[-1]
    flats = []
    for piece in pieces:
        flat = piece.reshape(-1, width)
        flats.append(jnp.pad(flat, ((0, -flat.shape[0] % 16), (0, 0))))
    signs = [(1, 1), (1, -1), (-1, 1), (-1, -1)]
    in_vmem = pl.BlockSpec(memory_space=pltpu.VMEM)
    results = pl.pallas_call(
        functools.partial(exchange_kernel, lat_steps, lon_steps),
        out_shape=[jax.ShapeDtypeStruct(flat.shape, flat.dtype) for flat in flats],
        in_specs=[in_vmem] * 3,
        out_specs=[in_vmem] * 3,
        scratch_shapes=[pltpu.SemaphoreType.DMA((3,)), pltpu.SemaphoreType.DMA((3,))],
        compiler_params=pltpu.CompilerParams(
            collective_id=4 * signs.index(lat_steps) + signs.index(lon_steps),
            has_side_effects=True,
            vmem_limit_bytes=8 * 1024 * 1024,
        ),
    )(*flats)
    return [out[: math.prod(piece.shape[:-1])].reshape(piece.shape) for out, piece in zip(results, pieces)]


def by_segment(make, steps):
    if steps[0] == steps[1]:
        return make(steps[0])
    return jnp.where(lax.axis_index("segment") == 0, make(steps[0]), make(steps[1]))


def neighbours(lat_steps, lon_steps, field):
    rows = lambda step: field[:, :HALF_LAT] if step > 0 else field[:, WLAT - HALF_LAT:]
    columns = lambda part: lambda step: part[:, :, :HALF_LON] if step > 0 else part[:, :, WLON - HALF_LON:]
    row_piece = by_segment(rows, lat_steps)
    corner_piece = by_segment(columns(row_piece), lon_steps)
    column_piece = by_segment(columns(field), lon_steps)
    return exchanged(lat_steps, lon_steps, (row_piece, corner_piece, column_piece))


def assembled(field, below, corner, beside, row, column):
    sliced = lax.dynamic_slice_in_dim
    near = jnp.concatenate([beside, field, beside], axis=2)
    near = sliced(near, column, field.shape[2], 2)
    far = jnp.concatenate([corner, below, corner], axis=2)
    far = sliced(far, column, field.shape[2], 2)
    tall = jnp.concatenate([far, near, far], axis=1)
    return sliced(tall, row, field.shape[1], 1)


def sign_of(lat_shift, lon_shift):
    return jnp.where(lat_shift < 0, 2, 0) + jnp.where(lon_shift < 0, 1, 0)


def plan_kernel(offsets_ref, *outs):
    lat_base = [based(offsets_ref[s, 0], WLAT) for s in (0, 1)]
    lon_base = [based(offsets_ref[s, 1], WLON) for s in (0, 1)]
    first = lax.axis_index("segment") == 0
    lat_step, lon_step = lat_base[1] - lat_base[0], lon_base[1] - lon_base[0]
    back = [sign_of(-lat_base[s], -lon_base[s]) for s in (0, 1)]
    numbers = (
        sign_of(lat_base[0], lon_base[0]),
        HALF_LAT + lat_base[0],
        HALF_LON + lon_base[0],
        sign_of(lat_step, lon_step),
        HALF_LAT + lat_step,
        HALF_LON + lon_step,
        jnp.where(back[1] > 0, 4 + back[1], back[0]),
        HALF_LAT - jnp.where(first, lat_base[0], lat_base[1]),
        HALF_LON - jnp.where(first, lon_base[0], lon_base[1]),
    )
    for out, number in zip(outs, numbers):
        out[0] = number


def planned(offsets):
    in_smem = pl.BlockSpec(memory_space=pltpu.SMEM)
    numbers = pl.pallas_call(
        plan_kernel,
        out_shape=[jax.ShapeDtypeStruct((1,), jnp.int32)] * 9,
        in_specs=[in_smem],
        out_specs=[in_smem] * 9,
    )(offsets)
    numbers = [number.reshape(()) for number in numbers]
    return numbers[:3], numbers[3:6], numbers[6:]


def shift(field, choice, row, column):
    ways = [functools.partial(neighbours, (a, a), (b, b)) for a in (1, -1) for b in (1, -1)]
    return assembled(field, *lax.switch(choice, ways, field), row, column)


def shift_each(field, choice, row, column):
    ways = []
    for segment in (0, 1):
        for a in (1, -1):
            for b in (1, -1):
                lat_steps = (a, 1) if segment == 0 else (1, a)
                lon_steps = (b, 1) if segment == 0 else (1, b)
                ways.append(functools.partial(neighbours, lat_steps, lon_steps))
    return assembled(field, *lax.switch(choice, ways, field), row, column)


def body(latents, land_mask, land_embed, qkv_weight, out_weight, norm_gain, offsets):
    segment_index = lax.axis_index("segment")
    assert latents.shape[1:3] == (WLAT, WLON)
    embedded = latents.astype(jnp.float32) + land_embed.astype(jnp.float32)
    seeded = jnp.where(land_mask[None, :, :, None] > 0, embedded, latents.astype(jnp.float32)).astype(jnp.bfloat16)
    wqkv = qkv_weight[0]
    wout = out_weight[0]
    into_first, into_second, back = planned(offsets)
    first_in = shift(seeded, *into_first)
    first, passed = attend(first_in, 0, offsets, wqkv, wout, norm_gain)
    passed = passed.reshape(latents.shape)
    second_in = shift(passed, *into_second)
    (second,) = attend(second_in, 1, offsets, wqkv, wout, norm_gain)
    merged = jnp.where(segment_index == 0, first, second).reshape(latents.shape)
    return shift_each(merged, *back)[None]


def solution(mesh):
    return jax.shard_map(
        body,
        mesh=mesh,
        in_specs=(
            P(None, "lat", "lon", None),
            P("lat", "lon"),
            P(),
            P("segment", None, None),
            P("segment", None, None),
            P(),
            P(),
        ),
        out_specs=P("segment", None, "lat", "lon", None),
        check_vma=False,
    )
```
